32 devices in a mesh: groups: 2 (over y), ep: 4 (over z), tp: 4 (over x, core).
Axes of the slice: x: 2, y: 2, z: 4, core: 2. Of those that a mesh axis runs over, the one named last changes fastest.
Arguments:
- queries: bfloat16 [192, 6144], P(('groups', 'ep'), 'tp'), parts along dimension 0, may hold values from -16 to 16
- cached_key_rows: bfloat16 [192, 128, 1024], P(('groups', 'ep'), None, 'tp'), parts along dimension 0, may hold values from -16 to 16
- cached_value_rows: bfloat16 [192, 128, 1024], P(('groups', 'ep'), None, 'tp'), parts along dimension 0, may hold values from -6 to 6
- lengths: int32 [192], P(('groups', 'ep')), parts along dimension 0, may hold values from 2 to 128, as said below
- out_weight: bfloat16 [6144, 6144], P('ep', 'tp'), may hold values from -0.078125 to 0.078125
- residual: bfloat16 [192, 6144], P(('groups', 'ep'), 'tp'), parts along dimension 0, may hold values from -6 to 6
- norm_gain: float32 [6144], P('tp'), may hold values from 0.5 to 2
- routes: int32 [192, 4], P(('groups', 'ep')), parts along dimension 0, may hold values from 0 to 15, all different within a row; in each aligned block of 24 rows (0 to 23, 24 to 47, ...) at most 14 rows name the same one
- route_gates: float32 [192, 4], P(('groups', 'ep')), parts along dimension 0, may hold values from 0.5 to 1.5
- gate_up_weight: bfloat16 [2, 6144, 2, 10752], P(None, 'tp', None, 'ep'), may hold values from -0.078125 to 0.078125
- down_weight: bfloat16 [2, 10752, 6144], P(None, 'ep', 'tp'), may hold values from -0.0625 to 0.0625
Outputs:
- mixed: bfloat16 [192, 6144], P(('groups', 'ep'), 'tp'), parts along dimension 0
The draws below stay inside these ranges and needn't reach their ends.
There are 2 independent parts, one for each index of `groups`. The reference program is written for one: setup_inputs(seed, part) draws one part's arguments, and reference() takes and returns one part's arrays. A program takes and returns all parts, laid end to end along the dimension named above; an argument that names none is the same for every part. Nothing has to cross between parts.
Inputs may be any that keep to these rules, and one draw needn't show every extreme that they name: `lengths`: some row has exactly 128 live positions. `routes`: each row names 4 different ids; in each aligned block of 24 rows no id is named by more than 14 rows, a bound that some block reaches.
All inputs are finite; a program needn't handle non-finite values.
Results may differ from the reference program's by a relative error of at most 0.015.
Values may be sent and summed in bfloat16 or wider, within the bound.
A program may use at most 192 MiB of HBM per device.

```python
import math
import jax
import jax.numpy as jnp
import numpy as np
from jax import lax

D = 6144
QUERY_HEAD_COUNT = 48
KEY_VALUE_HEADS = 8
HEAD_WIDTH = 128
FF = 10752
EXPERTS = 16
TOP = 4
EXP_WIN = 2
TOK_DEV = 24
CACHED_POSITIONS = 128
CAP = 14
BATCH_TOKENS = 96
N_EP = 4


def draw_queries(key, part):
    key = jax.random.fold_in(key, 11)
    value_rows = jnp.clip(jax.random.normal(key, (BATCH_TOKENS, QUERY_HEAD_COUNT, HEAD_WIDTH), jnp.float32), -6.0, 6.0)
    return value_rows.reshape(BATCH_TOKENS, QUERY_HEAD_COUNT * HEAD_WIDTH).astype(jnp.bfloat16)


def draw_cached_key_rows(key, part):
    key = jax.random.fold_in(key, 12)
    value_rows = jnp.clip(jax.random.normal(key, (BATCH_TOKENS, CACHED_POSITIONS, KEY_VALUE_HEADS, HEAD_WIDTH), jnp.float32), -6.0, 6.0)
    return value_rows.reshape(BATCH_TOKENS, CACHED_POSITIONS, KEY_VALUE_HEADS * HEAD_WIDTH).astype(jnp.bfloat16)


def draw_lengths(key, part):
    key = jax.random.fold_in(key, 13)
    drawn = jax.random.randint(key, (BATCH_TOKENS,), 2, CACHED_POSITIONS + 1, dtype=jnp.int32)
    longest = jax.random.randint(jax.random.fold_in(key, 1), (), 0, BATCH_TOKENS, dtype=jnp.int32)
    return drawn.at[longest].set(CACHED_POSITIONS)


def block_scale(own_key, dims, shards, least, largest):
    factor_of, own = 1.0, jax.random.fold_in(own_key, 6)
    for axis_at, parts in shards:
        heights = jnp.exp(jax.random.uniform(jax.random.fold_in(own, axis_at), (parts,), jnp.float32, least / len(shards), largest / len(shards)))
        factor_of = factor_of * jnp.repeat(heights, dims[axis_at] // parts).reshape([-1 if axis == axis_at else 1 for axis in range(len(dims))])
    return factor_of


def deal_out(key, own, number, rows, count, top, bound, skew):
    order = jax.random.permutation(key, count)
    packed, usual = portions_of(count, rows * top, bound, skew, True), portions_of(count, rows * top, bound, skew, False)
    places = jnp.arange(count)

    def named(sizes, rotation):
        used = int((sizes > 0).sum())
        fixed = max(1, used // 4)
        moved = fixed + (places - fixed + rotation * (used - fixed)) % max(1, count - fixed)
        return jnp.zeros((count,), jnp.int32).at[order[jnp.where(places < fixed, places, moved)]].set(jnp.asarray(sizes, jnp.int32))

    sizes = jnp.where(number % 4 == 0, named(packed, number // 4), named(usual, number - number // 4 - 1))
    mixed = jax.random.permutation(jax.random.fold_in(own, 3), count)
    giver, taker = mixed[0:count // 2 * 2:2], mixed[1:count // 2 * 2:2]
    margin = jnp.minimum(sizes[giver] - 1, bound - sizes[taker]) // 2
    margin = jnp.where((giver == order[0]) | (taker == order[0]) | (sizes[taker] == 0), 0, jnp.maximum(margin, 0))
    moved = jax.random.randint(jax.random.fold_in(own, 4), (count // 2,), 0, 1 << 20) % (margin + 1)
    sizes = sizes.at[giver].add(-moved).at[taker].add(moved)
    members = jnp.searchsorted(jnp.cumsum(sizes), jnp.arange(rows * top), side="right").astype(jnp.int32)
    grid = members.reshape(top, rows).T
    grid = grid[jax.random.permutation(jax.random.fold_in(own, 1), rows)]
    rotation = jax.random.randint(jax.random.fold_in(own, 2), (rows, 1), 0, top)
    return jnp.take_along_axis(grid, (jnp.arange(top)[None, :] + rotation) % top, axis=1)


def portions_of(count, total, reach, slope, full):
    portions = [(1 << 20) // math.isqrt(rank ** slope) + 1 for rank in range(1, count + 1)]
    largest = reach if full else min(reach, max(-(-total // count), total * portions[0] // sum(portions)))
    least = 1 if total - largest >= count - 1 else 0
    holding, spare = [largest] + [least] * (count - 1), total - largest - least * (count - 1)
    while spare > 0:
        candidates = [i for i in range(1, count) if holding[i] < largest] or [i for i in range(1, count) if holding[i] < reach]
        whole, budget = sum([portions[i] for i in candidates]), spare
        for i in candidates:
            addition = min(reach - holding[i], max(1, budget * portions[i] // whole), spare)
            holding[i] = holding[i] + addition
            spare = spare - addition
    return np.array(holding)


def centred(stream_key, extent, scale, bound, shards=(), kind=jnp.bfloat16):
    values = jax.random.normal(stream_key, extent, jnp.float32) * scale
    if len(shards) > 0:
        values = block_scale(stream_key, extent, shards, -0.22, 0.18) * values
    return jnp.clip(values, min=-bound, max=bound).astype(kind)


def setup_inputs(seed: int = 0, part: int = 0) -> dict:
    seeds = jax.random.split(jax.random.key(seed), 12)
    part_splits = jax.random.split(jax.random.fold_in(seeds[11], part), 12)
    queries = draw_queries(jax.random.fold_in(jax.random.fold_in(seeds[11], part), 71), part)
    cached_key_rows = draw_cached_key_rows(jax.random.fold_in(jax.random.fold_in(seeds[11], part), 71), part)
    cached_value_rows = centred(part_splits[2], (BATCH_TOKENS, CACHED_POSITIONS, KEY_VALUE_HEADS * HEAD_WIDTH), 1.0, 6.0, ((0, 4), (2, 4)))
    lengths = draw_lengths(jax.random.fold_in(jax.random.fold_in(seeds[11], part), 71), part)
    out_weight = centred(seeds[4], (QUERY_HEAD_COUNT * HEAD_WIDTH, D), (QUERY_HEAD_COUNT * HEAD_WIDTH) ** -0.5, 0.078125, ((0, 4), (1, 4)))
    residual = centred(part_splits[5], (BATCH_TOKENS, D), 1.0, 6.0, ((0, 4), (1, 4)))
    norm_gain = jnp.clip(jnp.exp(math.log(2.0) - 1.3862944 * jax.random.uniform(seeds[6], (D,), jnp.float32) ** block_scale(seeds[6], (D,), ((0, 4),), -0.2, 0.2)), 0.5, 2.0)
    routes_keys = jax.random.split(jax.random.fold_in(part_splits[7], 1), BATCH_TOKENS // TOK_DEV)
    routes_turns = jax.random.permutation(jax.random.fold_in(part_splits[7], 3), BATCH_TOKENS // TOK_DEV)
    routes = jax.vmap(lambda own, number: deal_out(jax.random.fold_in(part_splits[7], 2), own, number, TOK_DEV, EXPERTS, TOP, CAP, 2))(routes_keys, routes_turns).reshape((BATCH_TOKENS, TOP))
    route_gates = jnp.clip(0.5 + 1.0 * jax.random.uniform(part_splits[8], (BATCH_TOKENS, TOP), jnp.float32) ** block_scale(part_splits[8], (BATCH_TOKENS, TOP), ((0, 4),), -0.2, 0.2), 0.5, 1.5)
    gate_up_weight = centred(seeds[9], (EXP_WIN, D, 2, FF), D ** -0.5, 0.078125, ((1, 4), (3, 4)))
    down_weight = centred(seeds[10], (EXP_WIN, FF, D), FF ** -0.5, 0.0625, ((1, 4), (2, 4)))
    return {"queries": queries, "cached_key_rows": cached_key_rows, "cached_value_rows": cached_value_rows, "lengths": lengths, "out_weight": out_weight, "residual": residual, "norm_gain": norm_gain, "routes": routes, "route_gates": route_gates, "gate_up_weight": gate_up_weight, "down_weight": down_weight}


def attend(queries, cached_key_rows, cached_value_rows, lengths):
    query_group_width = QUERY_HEAD_COUNT // KEY_VALUE_HEADS
    per_head_queries = queries.astype(jnp.float32).reshape(BATCH_TOKENS, KEY_VALUE_HEADS, query_group_width, HEAD_WIDTH)
    per_head_keys = cached_key_rows.astype(jnp.float32).reshape(BATCH_TOKENS, CACHED_POSITIONS, KEY_VALUE_HEADS, HEAD_WIDTH)
    per_head_values = cached_value_rows.astype(jnp.float32).reshape(BATCH_TOKENS, CACHED_POSITIONS, KEY_VALUE_HEADS, HEAD_WIDTH)
    scores = jnp.einsum('tkgd,tskd->tkgs', per_head_queries, per_head_keys) * HEAD_WIDTH ** (-0.5)
    live = jnp.arange(CACHED_POSITIONS, dtype=jnp.int32)[None, :] < lengths[:, None]
    scores = jnp.where(live[:, None, None, :], scores, -1e+30)
    row_max = lax.optimization_barrier(jnp.max(scores, axis=-1, keepdims=True))
    expon = jnp.exp(scores - row_max)
    probs = (expon / lax.optimization_barrier(jnp.sum(expon, axis=-1, keepdims=True))).astype(jnp.bfloat16)
    weighted = jnp.einsum('tkgs,tskd->tkgd', probs.astype(jnp.float32), per_head_values)
    return weighted.astype(jnp.bfloat16).reshape(BATCH_TOKENS, QUERY_HEAD_COUNT * HEAD_WIDTH)

def expert_block(normed, routes, route_gates, gate_up_weight, down_weight, expert):
    chosen = jnp.any(routes == expert, axis=-1)
    chosen_int = chosen.astype(jnp.int32).reshape(N_EP, TOK_DEV)
    slot_index = (jnp.cumsum(chosen_int, axis=1) - chosen_int).reshape(BATCH_TOKENS)
    block_start = jnp.arange(BATCH_TOKENS, dtype=jnp.int32) // TOK_DEV * CAP
    filled = N_EP * CAP
    position = jnp.where(chosen, block_start + slot_index, filled).astype(jnp.int32)
    buffer = jnp.zeros((filled, D), normed.dtype).at[position].set(normed, mode='drop')
    gate_pre = jnp.dot(buffer, gate_up_weight[expert, :, 0, :], preferred_element_type=jnp.float32)
    up_pre = jnp.dot(buffer, gate_up_weight[expert, :, 1, :], preferred_element_type=jnp.float32)
    hidden = (jax.nn.silu(gate_pre) * up_pre).astype(jnp.bfloat16)
    width = FF // N_EP
    hidden_blocks = hidden.reshape(filled, N_EP, width).transpose(1, 0, 2)
    weight_blocks = down_weight[expert].reshape(N_EP, width, D)

    def add_block(total, pair):
        term = jnp.dot(pair[0], pair[1], preferred_element_type=jnp.float32).astype(jnp.bfloat16)
        term = lax.optimization_barrier(term)
        return (total + term.astype(jnp.float32), None)
    expert_out, _ = lax.scan(add_block, jnp.zeros((filled, D), jnp.float32), (hidden_blocks, weight_blocks))
    weight = lax.optimization_barrier(jnp.sum(jnp.where(routes == expert, route_gates, 0.0), axis=-1))
    picked = expert_out[jnp.minimum(position, filled - 1)]
    return jnp.where(chosen[:, None], weight[:, None] * picked, 0.0)

def reference(queries, cached_key_rows, cached_value_rows, lengths, out_weight, residual, norm_gain, routes, route_gates, gate_up_weight, down_weight):
    attended = attend(queries, cached_key_rows, cached_value_rows, lengths)
    projected = jnp.dot(attended, out_weight, preferred_element_type=jnp.float32)
    stream = residual.astype(jnp.float32) + projected
    scale = lax.rsqrt(lax.optimization_barrier(jnp.mean(stream * stream, axis=-1, keepdims=True)) + 1e-05)
    normed = (stream * scale * norm_gain).astype(jnp.bfloat16)
    total = stream
    for expert in range(EXP_WIN):
        total = total + expert_block(normed, routes, route_gates, gate_up_weight, down_weight, expert)
    return total.astype(jnp.bfloat16)
```

```python
import jax
import jax.numpy as jnp
from jax import lax
from jax.experimental import pallas as pl
from jax.experimental.pallas import tpu as pltpu
from jax.sharding import PartitionSpec as P

D = 6144
HEAD_WIDTH = 128
EXP_WIN = 2
CAP = 14


def local(
    queries,
    cached_key_rows,
    cached_value_rows,
    lengths,
    out_weight,
    residual,
    norm_gain,
    routes,
    route_gates,
    gate_up_weight,
    down_weight,
):
    row_count = queries.shape[0]
    head_count = queries.shape[1] // HEAD_WIDTH
    kv_count = cached_key_rows.shape[2] // HEAD_WIDTH
    query_group_width = head_count // kv_count
    cache_len = cached_key_rows.shape[1]
    per_head_queries = queries.reshape(row_count, kv_count, query_group_width, HEAD_WIDTH)
    per_head_keys = cached_key_rows.reshape(row_count, cache_len, kv_count, HEAD_WIDTH)
    per_head_values = cached_value_rows.reshape(row_count, cache_len, kv_count, HEAD_WIDTH)
    scores = jnp.einsum(
        "tkgd,tskd->tkgs", per_head_queries, per_head_keys, preferred_element_type=jnp.float32
    ) * HEAD_WIDTH ** (-0.5)
    live = jnp.arange(cache_len, dtype=jnp.int32)[None, :] < lengths[:, None]
    scores = jnp.where(live[:, None, None, :], scores, -1e30)
    row_max = jnp.max(scores, axis=-1, keepdims=True)
    expon = jnp.exp(scores - row_max)
    probs = (expon / jnp.sum(expon, axis=-1, keepdims=True)).astype(jnp.bfloat16)
    weighted = jnp.einsum(
        "tkgs,tskd->tkgd", probs, per_head_values, preferred_element_type=jnp.float32
    )
    attended = weighted.astype(jnp.bfloat16).reshape(row_count, head_count * HEAD_WIDTH)
    full_rows = lax.all_gather(attended, "tp", axis=1, tiled=True)
    feature_slices = lax.all_to_all(full_rows, "ep", split_axis=1, concat_axis=0, tiled=True)
    projected = lax.psum_scatter(
        jnp.dot(feature_slices, out_weight, preferred_element_type=jnp.float32).astype(
            jnp.bfloat16
        ),
        "ep",
        scatter_dimension=0,
        tiled=True,
    ).astype(jnp.float32)
    stream = residual.astype(jnp.float32) + projected
    square_total = lax.psum(jnp.sum(stream * stream, axis=-1), "tp")
    normed = (stream * lax.rsqrt(square_total[:, None] / D + 1e-05) * norm_gain[None, :]).astype(
        jnp.bfloat16
    )
    expert_ids = jnp.arange(EXP_WIN, dtype=jnp.int32)
    matches = routes[:, :, None] == expert_ids[None, None, :]
    chosen = jnp.any(matches, axis=1)
    chosen_int = chosen.astype(jnp.int32)
    slot_index = jnp.cumsum(chosen_int, axis=0) - chosen_int
    slot_ids = jnp.arange(CAP, dtype=jnp.int32)[:, None, None]
    placement_map = (chosen[None, :, :] & (slot_index[None, :, :] == slot_ids)).astype(jnp.float32)
    buffers = jnp.einsum(
        "cte,td->ced",
        placement_map.astype(jnp.bfloat16),
        normed,
        preferred_element_type=jnp.float32,
    ).astype(jnp.bfloat16)
    partial_pre = jnp.einsum(
        "ced,edgf->cegf",
        lax.all_gather(buffers, "ep", axis=0, tiled=True),
        gate_up_weight,
        preferred_element_type=jnp.float32,
    )
    summed = lax.psum(partial_pre.astype(jnp.bfloat16), "tp").astype(jnp.float32)
    hidden = (jax.nn.silu(summed[:, :, 0]) * summed[:, :, 1]).astype(jnp.bfloat16)
    expert_out = lax.psum_scatter(
        jnp.einsum("cef,efd->ced", hidden, down_weight, preferred_element_type=jnp.float32).astype(
            jnp.bfloat16
        ),
        "ep",
        scatter_dimension=0,
        tiled=True,
    ).astype(jnp.float32)
    gate_weights = jnp.sum(route_gates[:, :, None] * matches.astype(jnp.float32), axis=1)
    combined = jnp.einsum(
        "cte,ced->td",
        placement_map * gate_weights[None, :, :],
        expert_out,
        precision=lax.Precision.HIGHEST,
    )
    return (stream + combined).astype(jnp.bfloat16)


MESH = pl.DeviceIdType.MESH
ROWS = 24
PAIR = 2 * ROWS
HALF = 768
N = 4
SLOTS = N * CAP
LANE = 128
TILES = 21
SIDE = 11
STEP = 10
WIDE = SIDE * LANE
K = 2 * HALF


def bf(x):
    return x.astype(jnp.bfloat16)


def f32(x):
    return x.astype(jnp.float32)


def mm(a, b):
    return jnp.dot(a, b, preferred_element_type=jnp.float32)


def fused(
    att_ref,
    meta_ref,
    res_ref,
    gain_ref,
    wo_hbm,
    gu_hbm,
    wd_hbm,
    out_ref,
    wo,
    gu,
    wd,
    a_send,
    a_recv,
    part,
    rs_send,
    rs_recv,
    meta_all,
    y_all,
    ss_all,
    stream,
    xp,
    s_mine,
    s_recv,
    l1_send,
    l1_recv,
    acc,
    l2_send,
    l2_recv,
    hid,
    outs,
    c_send,
    c_recv,
    wo_sem,
    gu_sem,
    wd_sem,
    a_ss,
    a_rs,
    m_ss,
    m_rs,
    rs_ss,
    rs_rs,
    y_ss,
    y_rs,
    q_ss,
    q_rs,
    s_ss,
    s_rs,
    l1_ss,
    l1_rs,
    l2_ss,
    l2_rs,
    h_ss,
    h_rs,
    c_ss,
    c_rs,
):
    g, i, j = lax.axis_index("groups"), lax.axis_index("ep"), lax.axis_index("tp")
    x, c = j // 2, j % 2
    sibling = (g, i, x * 2 + (1 - c))
    across = (g, i, (1 - x) * 2 + c)

    def remote(src, dst, ss, rs, dev):
        return pltpu.make_async_remote_copy(
            src_ref=src, dst_ref=dst, send_sem=ss, recv_sem=rs, device_id=dev, device_id_type=MESH
        )

    barrier = pltpu.get_barrier_semaphore()
    me = i * N + j
    for d in range(1, N * N):
        other = (me + d) % (N * N)
        pl.semaphore_signal(
            barrier, inc=1, device_id=(g, other // N, other % N), device_id_type=MESH
        )

    wo_copy = pltpu.make_async_copy(wo_hbm, wo, wo_sem)
    wo_copy.start()

    def gu_copy(e, t):
        return pltpu.make_async_copy(
            gu_hbm.at[e, :, :, pl.ds(pl.multiple_of(t * LANE, LANE), LANE)],
            gu.at[e * TILES + t],
            gu_sem.at[e * TILES + t],
        )

    def wd_copy(e):
        return pltpu.make_async_copy(wd_hbm.at[e], wd.at[e], wd_sem.at[e])

    a_send[0:ROWS, :] = att_ref[:, 0:HALF]
    a_send[ROWS:PAIR, :] = att_ref[:, HALF:K]
    meta_all[i] = meta_ref[...]

    pl.semaphore_wait(barrier, N * N - 1)

    for d in (1, 2, 3):
        remote(a_send, a_recv.at[i], a_ss.at[d], a_rs.at[i], (g, j, (j + d) % N)).start()

    @pl.when(i != j)
    def _():
        remote(a_send, a_recv.at[i], a_ss.at[0], a_rs.at[i], (g, j, j)).start()

    @pl.when(i == j)
    def _():
        a_recv[i] = a_send[...]

    for d in (1, 2, 3):
        remote(
            meta_all.at[i], meta_all.at[i], m_ss.at[d], m_rs.at[i], (g, (i + d) % N, j)
        ).start()

    for e in (1 - c, c):

        @pl.loop(0, TILES)
        def _(t, e=e):
            gu_copy(e, t).start()

    for e in range(EXP_WIN):
        wd_copy(e).start()

    for d in range(N):
        s = (i + d) % N

        @pl.when(jnp.logical_or(d != 0, i != j))
        def _(s=s):
            remote(a_send, a_recv.at[s], a_ss.at[0], a_rs.at[s], sibling).wait_recv()

    wo_copy.wait()
    lhs = [
        jnp.concatenate([a_recv[k, ROWS * h : ROWS * (h + 1), :] for k in range(N)], axis=0)
        for h in range(2)
    ]
    for n in range(2):
        cols = slice(HALF * n, HALF * (n + 1))
        r = mm(lhs[0], wo[0:HALF, cols]) + mm(lhs[1], wo[HALF:K, cols])
        part[:, cols] = r
        for k in range(N):
            rs_send[k, ROWS * n : ROWS * (n + 1), :] = bf(r[ROWS * k : ROWS * (k + 1), :])
    for d in (2, 1, 3):
        k = (i + d) % N
        remote(rs_send.at[k], rs_recv.at[i], rs_ss.at[d], rs_rs.at[i], (g, k, j)).start()
    mine = pl.ds(pl.multiple_of(i * ROWS, 8), ROWS)
    stream[...] = f32(res_ref[...]) + part[mine, :]
    for d in (1, 3, 2):
        s = (i + d) % N
        remote(rs_send.at[s], rs_recv.at[s], rs_ss.at[d], rs_rs.at[s], sibling).wait_recv()
        got = f32(rs_recv[s])
        stream[:, 0:HALF] += got[0:ROWS]
        stream[:, HALF:K] += got[ROWS:PAIR]

    st = stream[...]
    y = bf(st * gain_ref[...])
    y_all[i] = jnp.concatenate([y[:, 0:HALF], y[:, HALF:K]], axis=0)
    ss_all[i] = jnp.broadcast_to(jnp.sum(st * st, axis=1, keepdims=True), (ROWS, LANE))
    for d in (2, 1, 3):
        dev = (g, (i + d) % N, j)
        remote(y_all.at[i], y_all.at[i], y_ss.at[d], y_rs.at[i], dev).start()
        remote(ss_all.at[i], ss_all.at[i], q_ss.at[d], q_rs.at[i], dev).start()
    for d in (1, 3, 2):
        s = (i + d) % N
        remote(meta_all.at[s], meta_all.at[s], m_ss.at[d], m_rs.at[s], sibling).wait_recv()
        remote(ss_all.at[s], ss_all.at[s], q_ss.at[d], q_rs.at[s], sibling).wait_recv()
        remote(y_all.at[s], y_all.at[s], y_ss.at[d], y_rs.at[s], sibling).wait_recv()

    ydat = [
        jnp.concatenate([y_all[k, ROWS * h : ROWS * (h + 1), :] for k in range(N)], axis=0)
        for h in range(2)
    ]
    ssd = jnp.concatenate([ss_all[k] for k in range(N)], axis=0)
    twice = bf(
        lax.broadcasted_iota(jnp.int32, (LANE, 2 * LANE), 1) // 2
        == lax.broadcasted_iota(jnp.int32, (LANE, 2 * LANE), 0)
    )
    keep = (
        lax.broadcasted_iota(jnp.int32, (2 * SLOTS, 2 * LANE), 1) % 2
        == lax.broadcasted_iota(jnp.int32, (2 * SLOTS, 2 * LANE), 0) // SLOTS
    )

    def spots(e):
        return jnp.concatenate(
            [meta_all[k, ROWS * e : ROWS * (e + 1), :] for k in range(N)], axis=0
        )

    for e in range(EXP_WIN):
        place = spots(e)
        place_t = jnp.transpose(
            jnp.concatenate([place, jnp.zeros((LANE - N * ROWS, LANE), jnp.float32)], axis=0)
        )[0 : 2 * SLOTS, 0 : N * ROWS]
        s_mine[e] = jnp.dot(
            place_t, ssd, precision=lax.Precision.HIGHEST, preferred_element_type=jnp.float32
        )
        place_b = bf(place_t)
        for h in range(2):
            rows = bf(mm(place_b, ydat[h]))
            for q in range(HALF // LANE):
                both = mm(rows[:, LANE * q : LANE * (q + 1)], twice)
                at = 2 * (HALF * h + LANE * q)
                xp[e, :, at : at + 2 * LANE] = bf(jnp.where(keep, both, 0.0))

    s_one = remote(s_mine.at[1 - c], s_recv.at[0], s_ss.at[0], s_rs.at[0], sibling)
    s_one.start()

    def product(e, h, p, width):
        t = e * TILES + h * STEP + 2 * p
        w = [gu.at[t + k].reshape(2 * K, LANE)[...] for k in range(width)]
        w = w[0] if width == 1 else jnp.concatenate(w, axis=1)
        return mm(xp[e], w)

    def sweep(e, h, store):
        @pl.loop(0, SIDE // 2)
        def _(p):
            at = pl.ds(pl.multiple_of(p * 2 * LANE, 2 * LANE), 2 * LANE)
            store(at, product(e, h, p, 2))

        store(pl.ds((SIDE - 1) * LANE, LANE), product(e, h, SIDE // 2, 1))

    def arrive(e):
        @pl.loop(0, TILES)
        def _(t):
            gu_copy(e, t).wait()

    arrive(1 - c)
    for n, h in enumerate((1 - x, x)):

        def to_sibling(at, r, n=n):
            l1_send[n, :, at] = bf(r)

        sweep(1 - c, h, to_sibling)
        remote(l1_send.at[n], l1_recv.at[n], l1_ss.at[n], l1_rs.at[n], sibling).start()
    arrive(c)
    s_one.wait_recv()
    s_mine[c] = s_mine[c] + s_recv[0]
    s_two = remote(s_mine.at[c], s_recv.at[1], s_ss.at[1], s_rs.at[1], across)
    s_two.start()
    first = remote(l1_send.at[0], l1_recv.at[0], l1_ss.at[0], l1_rs.at[0], sibling)
    first.wait_recv()

    def to_across(at, r):
        l2_send[:, at] = bf(r + f32(l1_recv[0, :, at]))

    sweep(c, 1 - x, to_across)
    l2 = remote(l2_send, l2_recv, l2_ss, l2_rs, across)
    l2.start()
    second = remote(l1_send.at[1], l1_recv.at[1], l1_ss.at[1], l1_rs.at[1], sibling)
    second.wait_recv()

    def to_own(at, r):
        acc[:, at] = r + f32(l1_recv[1, :, at])

    sweep(c, x, to_own)
    s_two.wait_recv()
    scale = lax.rsqrt((s_mine[c] + s_recv[1])[0:SLOTS, 0:1] / D + 1e-05)
    l2.wait_recv()

    @pl.loop(0, SIDE)
    def _(t):
        at = pl.ds(pl.multiple_of(t * LANE, LANE), LANE)
        total = acc[:, at] + f32(l2_recv[:, at])
        gate, up = total[0:SLOTS] * scale, total[SLOTS : 2 * SLOTS] * scale
        value = gate / (1.0 + jnp.exp(-gate)) * up
        value = jnp.where(jnp.logical_and(t == 0, x == 1), 0.0, value)
        hid[c, x, :, at] = bf(
            jnp.concatenate([value, jnp.zeros((64 - SLOTS, LANE), jnp.float32)], axis=0)
        )

    h_sib = remote(hid.at[c, x], hid.at[c, x], h_ss.at[0], h_rs.at[0], sibling)
    h_acr = remote(hid.at[c, x], hid.at[c, x], h_ss.at[1], h_rs.at[1], across)
    h_acr.start()
    h_sib.start()
    for e in range(EXP_WIN):
        wd_copy(e).wait()

    def down(e, h, n):
        rows = pl.ds(pl.multiple_of(h * STEP * LANE, LANE), WIDE)
        return mm(hid[e, h], wd[e, rows, 512 * n : 512 * (n + 1)])

    for n in range(3):
        outs[c, :, 512 * n : 512 * (n + 1)] = down(c, x, n)
    h_sib.wait_recv()
    for n in range(3):
        outs[1 - c, :, 512 * n : 512 * (n + 1)] = down(1 - c, x, n)
    h_acr.wait_recv()
    h_fwd = remote(hid.at[c, 1 - x], hid.at[c, 1 - x], h_ss.at[2], h_rs.at[2], sibling)
    h_fwd.start()
    for n in range(3):
        outs[c, :, 512 * n : 512 * (n + 1)] += down(c, 1 - x, n)
    h_fwd.wait_recv()
    for n in range(3):
        outs[1 - c, :, 512 * n : 512 * (n + 1)] += down(1 - c, 1 - x, n)

    gates = jnp.concatenate([meta_all[k, 2 * ROWS : 3 * ROWS, :] for k in range(N)], axis=0)
    live = lax.broadcasted_iota(jnp.int32, (N * ROWS, 64), 1) < SLOTS
    picks = [bf(jnp.where(live, spots(e)[:, 0:64], 0.0)) for e in range(EXP_WIN)]
    for n in range(2):
        cols = slice(HALF * n, HALF * (n + 1))
        r = gates[:, 0:1] * mm(picks[0], bf(outs[0, :, cols]))
        r = r + gates[:, 1:2] * mm(picks[1], bf(outs[1, :, cols]))
        part[:, cols] = r
        for k in range(N):
            c_send[k, ROWS * n : ROWS * (n + 1), :] = bf(r[ROWS * k : ROWS * (k + 1), :])
    for d in (2, 1, 3):
        k = (i + d) % N
        remote(c_send.at[k], c_recv.at[i], c_ss.at[d], c_rs.at[i], (g, k, j)).start()
    stream[...] += part[mine, :]
    for d in (1, 3, 2):
        s = (i + d) % N
        remote(c_send.at[s], c_recv.at[s], c_ss.at[d], c_rs.at[s], sibling).wait_recv()
        got = f32(c_recv[s])
        stream[:, 0:HALF] += got[0:ROWS]
        stream[:, HALF:K] += got[ROWS:PAIR]
    out_ref[...] = bf(stream[...])

    for d in (1, 2, 3):
        remote(a_send, a_recv.at[i], a_ss.at[d], a_rs.at[i], sibling).wait_send()
        remote(meta_all.at[i], meta_all.at[i], m_ss.at[d], m_rs.at[i], sibling).wait_send()
        k = (i + d) % N
        remote(rs_send.at[k], rs_recv.at[i], rs_ss.at[d], rs_rs.at[i], sibling).wait_send()
        remote(y_all.at[i], y_all.at[i], y_ss.at[d], y_rs.at[i], sibling).wait_send()
        remote(ss_all.at[i], ss_all.at[i], q_ss.at[d], q_rs.at[i], sibling).wait_send()
        remote(c_send.at[k], c_recv.at[i], c_ss.at[d], c_rs.at[i], sibling).wait_send()

    @pl.when(i != j)
    def _():
        remote(a_send, a_recv.at[i], a_ss.at[0], a_rs.at[i], sibling).wait_send()

    for copy in (s_one, s_two, first, second, l2, h_sib, h_acr, h_fwd):
        copy.wait_send()


def attention(queries, cached_key_rows, cached_value_rows, lengths):
    row_count = queries.shape[0]
    head_count = queries.shape[1] // HEAD_WIDTH
    kv_count = cached_key_rows.shape[2] // HEAD_WIDTH
    query_group_width = head_count // kv_count
    cache_len = cached_key_rows.shape[1]
    per_head_queries = queries.reshape(row_count, kv_count, query_group_width, HEAD_WIDTH)
    per_head_keys = cached_key_rows.reshape(row_count, cache_len, kv_count, HEAD_WIDTH)
    per_head_values = cached_value_rows.reshape(row_count, cache_len, kv_count, HEAD_WIDTH)
    scores = jnp.einsum(
        "tkgd,tskd->tkgs", per_head_queries, per_head_keys, preferred_element_type=jnp.float32
    ) * HEAD_WIDTH ** (-0.5)
    live = jnp.arange(cache_len, dtype=jnp.int32)[None, :] < lengths[:, None]
    scores = jnp.where(live[:, None, None, :], scores, -1e30)
    row_max = jnp.max(scores, axis=-1, keepdims=True)
    expon = jnp.exp(scores - row_max)
    probs = (expon / jnp.sum(expon, axis=-1, keepdims=True)).astype(jnp.bfloat16)
    weighted = jnp.einsum(
        "tkgs,tskd->tkgd", probs, per_head_values, preferred_element_type=jnp.float32
    )
    return weighted.astype(jnp.bfloat16).reshape(row_count, head_count * HEAD_WIDTH)


def placement(routes, route_gates):
    matches = routes[:, :, None] == jnp.arange(EXP_WIN, dtype=jnp.int32)[None, None, :]
    chosen = jnp.any(matches, axis=1)
    earlier = jnp.arange(ROWS)[:, None] > jnp.arange(ROWS)[None, :]
    slot = jnp.sum(earlier[:, :, None] & chosen[None, :, :], axis=1, dtype=jnp.int32)
    position = jnp.where(chosen, lax.axis_index("ep") * CAP + slot, -1)
    lanes = jnp.arange(LANE, dtype=jnp.int32)
    lanes = jnp.where(lanes < 2 * SLOTS, lanes % SLOTS, -2)
    spots = (position.T[:, :, None] == lanes[None, None, :]).astype(jnp.float32)
    gates = jnp.sum(route_gates[:, :, None] * matches.astype(jnp.float32), axis=1)
    gates = jnp.pad(gates, ((0, 0), (0, LANE - EXP_WIN)))
    return jnp.concatenate([spots.reshape(EXP_WIN * ROWS, LANE), gates], axis=0)


def fused_local(
    queries,
    cached_key_rows,
    cached_value_rows,
    lengths,
    out_weight,
    residual,
    norm_gain,
    routes,
    route_gates,
    gate_up_weight,
    down_weight,
):
    attended = attention(queries, cached_key_rows, cached_value_rows, lengths)
    meta = placement(routes, route_gates)
    b16, f4 = jnp.bfloat16, jnp.float32
    vmem, hbm = pl.BlockSpec(memory_space=pltpu.VMEM), pl.BlockSpec(memory_space=pl.ANY)
    dma = pltpu.SemaphoreType.DMA
    scratch = [
        pltpu.VMEM((K, K), b16),
        pltpu.VMEM((EXP_WIN * TILES, K, 2, LANE), b16),
        pltpu.VMEM((EXP_WIN, TILES * LANE, K), b16),
        pltpu.VMEM((PAIR, HALF), b16),
        pltpu.VMEM((N, PAIR, HALF), b16),
        pltpu.VMEM((N * ROWS, K), f4),
        pltpu.VMEM((N, PAIR, HALF), b16),
        pltpu.VMEM((N, PAIR, HALF), b16),
        pltpu.VMEM((N, 3 * ROWS, LANE), f4),
        pltpu.VMEM((N, PAIR, HALF), b16),
        pltpu.VMEM((N, ROWS, LANE), f4),
        pltpu.VMEM((ROWS, K), f4),
        pltpu.VMEM((EXP_WIN, 2 * SLOTS, 2 * K), b16),
        pltpu.VMEM((EXP_WIN, 2 * SLOTS, LANE), f4),
        pltpu.VMEM((2, 2 * SLOTS, LANE), f4),
        pltpu.VMEM((2, 2 * SLOTS, WIDE), b16),
        pltpu.VMEM((2, 2 * SLOTS, WIDE), b16),
        pltpu.VMEM((2 * SLOTS, WIDE), f4),
        pltpu.VMEM((2 * SLOTS, WIDE), b16),
        pltpu.VMEM((2 * SLOTS, WIDE), b16),
        pltpu.VMEM((EXP_WIN, 2, 64, WIDE), b16),
        pltpu.VMEM((EXP_WIN, 64, K), f4),
        pltpu.VMEM((N, PAIR, HALF), b16),
        pltpu.VMEM((N, PAIR, HALF), b16),
        dma,
        dma((EXP_WIN * TILES,)),
        dma((EXP_WIN,)),
    ]
    scratch += [dma((N,))] * 10 + [dma((2,))] * 4 + [dma, dma] + [dma((3,))] * 2 + [dma((N,))] * 2
    return pl.pallas_call(
        fused,
        out_shape=jax.ShapeDtypeStruct((ROWS, K), b16),
        in_specs=[vmem] * 4 + [hbm] * 3,
        out_specs=vmem,
        scratch_shapes=scratch,
        compiler_params=pltpu.CompilerParams(
            collective_id=0, has_side_effects=True, vmem_limit_bytes=VMEM_BYTES
        ),
    )(attended, meta, residual, norm_gain[None, :], out_weight, gate_up_weight, down_weight)


VMEM_BYTES = 63 << 20


def pick(mesh):
    fits = mesh.shape["ep"] == N and mesh.shape["tp"] == N
    return fused_local if fits else local


def solution(mesh):
    in_specs = (
        P(("groups", "ep"), "tp"),
        P(("groups", "ep"), None, "tp"),
        P(("groups", "ep"), None, "tp"),
        P(("groups", "ep")),
        P("ep", "tp"),
        P(("groups", "ep"), "tp"),
        P("tp"),
        P(("groups", "ep"), None),
        P(("groups", "ep"), None),
        P(None, "tp", None, "ep"),
        P(None, "ep", "tp"),
    )
    out_specs = P(("groups", "ep"), "tp")
    return jax.shard_map(pick(mesh), mesh=mesh, in_specs=in_specs, out_specs=out_specs, check_vma=False)
```

```python
import jax
import jax.numpy as jnp
from jax import lax
from jax.experimental import pallas as pl
from jax.experimental.pallas import tpu as pltpu
from jax.sharding import PartitionSpec as P

D = 6144
HEAD_WIDTH = 128
EXP_WIN = 2
CAP = 14


def local(
    queries,
    cached_key_rows,
    cached_value_rows,
    lengths,
    out_weight,
    residual,
    norm_gain,
    routes,
    route_gates,
    gate_up_weight,
    down_weight,
):
    row_count = queries.shape[0]
    head_count = queries.shape[1] // HEAD_WIDTH
    kv_count = cached_key_rows.shape[2] // HEAD_WIDTH
    query_group_width = head_count // kv_count
    cache_len = cached_key_rows.shape[1]
    per_head_queries = queries.reshape(row_count, kv_count, query_group_width, HEAD_WIDTH)
    per_head_keys = cached_key_rows.reshape(row_count, cache_len, kv_count, HEAD_WIDTH)
    per_head_values = cached_value_rows.reshape(row_count, cache_len, kv_count, HEAD_WIDTH)
    scores = jnp.einsum(
        "tkgd,tskd->tkgs", per_head_queries, per_head_keys, preferred_element_type=jnp.float32
    ) * HEAD_WIDTH ** (-0.5)
    live = jnp.arange(cache_len, dtype=jnp.int32)[None, :] < lengths[:, None]
    scores = jnp.where(live[:, None, None, :], scores, -1e30)
    row_max = jnp.max(scores, axis=-1, keepdims=True)
    expon = jnp.exp(scores - row_max)
    probs = (expon / jnp.sum(expon, axis=-1, keepdims=True)).astype(jnp.bfloat16)
    weighted = jnp.einsum(
        "tkgs,tskd->tkgd", probs, per_head_values, preferred_element_type=jnp.float32
    )
    attended = weighted.astype(jnp.bfloat16).reshape(row_count, head_count * HEAD_WIDTH)
    full_rows = lax.all_gather(attended, "tp", axis=1, tiled=True)
    feature_slices = lax.all_to_all(full_rows, "ep", split_axis=1, concat_axis=0, tiled=True)
    projected = lax.psum_scatter(
        jnp.dot(feature_slices, out_weight, preferred_element_type=jnp.float32).astype(
            jnp.bfloat16
        ),
        "ep",
        scatter_dimension=0,
        tiled=True,
    ).astype(jnp.float32)
    stream = residual.astype(jnp.float32) + projected
    square_total = lax.psum(jnp.sum(stream * stream, axis=-1), "tp")
    normed = (stream * lax.rsqrt(square_total[:, None] / D + 1e-05) * norm_gain[None, :]).astype(
        jnp.bfloat16
    )
    expert_ids = jnp.arange(EXP_WIN, dtype=jnp.int32)
    matches = routes[:, :, None] == expert_ids[None, None, :]
    chosen = jnp.any(matches, axis=1)
    chosen_int = chosen.astype(jnp.int32)
    slot_index = jnp.cumsum(chosen_int, axis=0) - chosen_int
    slot_ids = jnp.arange(CAP, dtype=jnp.int32)[:, None, None]
    placement_map = (chosen[None, :, :] & (slot_index[None, :, :] == slot_ids)).astype(jnp.float32)
    buffers = jnp.einsum(
        "cte,td->ced",
        placement_map.astype(jnp.bfloat16),
        normed,
        preferred_element_type=jnp.float32,
    ).astype(jnp.bfloat16)
    partial_pre = jnp.einsum(
        "ced,edgf->cegf",
        lax.all_gather(buffers, "ep", axis=0, tiled=True),
        gate_up_weight,
        preferred_element_type=jnp.float32,
    )
    summed = lax.psum(partial_pre.astype(jnp.bfloat16), "tp").astype(jnp.float32)
    hidden = (jax.nn.silu(summed[:, :, 0]) * summed[:, :, 1]).astype(jnp.bfloat16)
    expert_out = lax.psum_scatter(
        jnp.einsum("cef,efd->ced", hidden, down_weight, preferred_element_type=jnp.float32).astype(
            jnp.bfloat16
        ),
        "ep",
        scatter_dimension=0,
        tiled=True,
    ).astype(jnp.float32)
    gate_weights = jnp.sum(route_gates[:, :, None] * matches.astype(jnp.float32), axis=1)
    combined = jnp.einsum(
        "cte,ced->td",
        placement_map * gate_weights[None, :, :],
        expert_out,
        precision=lax.Precision.HIGHEST,
    )
    return (stream + combined).astype(jnp.bfloat16)


MESH = pl.DeviceIdType.MESH
ROWS = 24
PAIR = 2 * ROWS
HALF = 768
N = 4
SLOTS = N * CAP
LANE = 128
TILES = 21
SIDE = 11
STEP = 10
WIDE = SIDE * LANE
K = 2 * HALF


def bf(x):
    return x.astype(jnp.bfloat16)


def f32(x):
    return x.astype(jnp.float32)


def mm(a, b):
    return jnp.dot(a, b, preferred_element_type=jnp.float32)


def fused(
    att_ref,
    meta_ref,
    res_ref,
    gain_ref,
    wo_hbm,
    gu_hbm,
    wd_hbm,
    out_ref,
    wo,
    gu,
    wd,
    a_send,
    a_recv,
    part,
    rs_send,
    rs_recv,
    meta_all,
    y_all,
    ss_all,
    stream,
    xp,
    s_mine,
    s_recv,
    l1_send,
    l1_recv,
    acc,
    l2_send,
    l2_recv,
    hid,
    outs,
    c_send,
    c_recv,
    wo_sem,
    gu_sem,
    wd_sem,
    a_ss,
    a_rs,
    m_ss,
    m_rs,
    rs_ss,
    rs_rs,
    y_ss,
    y_rs,
    q_ss,
    q_rs,
    s_ss,
    s_rs,
    l1_ss,
    l1_rs,
    l2_ss,
    l2_rs,
    hs_ss,
    hs_rs,
    h_ss,
    h_rs,
    f_ss,
    f_rs,
    c_ss,
    c_rs,
):
    g, i, j = lax.axis_index("groups"), lax.axis_index("ep"), lax.axis_index("tp")
    x, c = j // 2, j % 2
    sibling = (g, i, x * 2 + (1 - c))
    across = (g, i, (1 - x) * 2 + c)

    def remote(src, dst, ss, rs, dev):
        return pltpu.make_async_remote_copy(
            src_ref=src, dst_ref=dst, send_sem=ss, recv_sem=rs, device_id=dev, device_id_type=MESH
        )

    barrier = pltpu.get_barrier_semaphore()
    me = i * N + j
    for d in range(1, N * N):
        other = (me + d) % (N * N)
        pl.semaphore_signal(
            barrier, inc=1, device_id=(g, other // N, other % N), device_id_type=MESH
        )

    wo_copy = pltpu.make_async_copy(wo_hbm, wo, wo_sem)
    wo_copy.start()
    gu_flat = gu_hbm.reshape(EXP_WIN * 2 * K, TILES * LANE)

    def gu_copy(e, t):
        return pltpu.make_async_copy(
            gu_flat.at[
                pl.ds(pl.multiple_of(e * 2 * K, 2 * K), 2 * K),
                pl.ds(pl.multiple_of(t * LANE, LANE), LANE),
            ],
            gu.at[e * TILES + t],
            gu_sem.at[e * TILES + t],
        )

    def wd_copy(e):
        return pltpu.make_async_copy(wd_hbm.at[e], wd.at[e], wd_sem.at[e])

    for e in (1 - c, c):

        @pl.loop(0, TILES)
        def _(t, e=e):
            gu_copy(e, t).start()

    for e in range(EXP_WIN):
        wd_copy(e).start()

    a_send[0:ROWS, :] = att_ref[:, 0:HALF]
    a_send[ROWS:PAIR, :] = att_ref[:, HALF:K]
    meta_all[i] = meta_ref[...]

    pl.semaphore_wait(barrier, N * N - 1)

    for d in (1, 2, 3):
        remote(a_send, a_recv.at[i], a_ss.at[d], a_rs.at[i], (g, j, (j + d) % N)).start()

    @pl.when(i != j)
    def _():
        remote(a_send, a_recv.at[i], a_ss.at[0], a_rs.at[i], (g, j, j)).start()

    @pl.when(i == j)
    def _():
        a_recv[i] = a_send[...]

    for d in (1, 2, 3):
        remote(
            meta_all.at[i], meta_all.at[i], m_ss.at[d], m_rs.at[i], (g, (i + d) % N, j)
        ).start()

    for d in range(N):
        s = (i + d) % N

        @pl.when(jnp.logical_or(d != 0, i != j))
        def _(s=s):
            remote(a_send, a_recv.at[s], a_ss.at[0], a_rs.at[s], sibling).wait_recv()

    wo_copy.wait()
    lhs = [
        jnp.concatenate([a_recv[k, ROWS * h : ROWS * (h + 1), :] for k in range(N)], axis=0)
        for h in range(2)
    ]
    for n in range(2):
        cols = slice(HALF * n, HALF * (n + 1))
        r = mm(lhs[0], wo[0:HALF, cols]) + mm(lhs[1], wo[HALF:K, cols])
        part[:, cols] = r
        for k in range(N):
            rs_send[k, ROWS * n : ROWS * (n + 1), :] = bf(r[ROWS * k : ROWS * (k + 1), :])
    for d in (2, 1, 3):
        k = (i + d) % N
        remote(rs_send.at[k], rs_recv.at[i], rs_ss.at[d], rs_rs.at[i], (g, k, j)).start()
    mine = pl.ds(pl.multiple_of(i * ROWS, 8), ROWS)
    stream[...] = f32(res_ref[...]) + part[mine, :]
    for d in (1, 3, 2):
        s = (i + d) % N
        remote(rs_send.at[s], rs_recv.at[s], rs_ss.at[d], rs_rs.at[s], sibling).wait_recv()
        got = f32(rs_recv[s])
        stream[:, 0:HALF] += got[0:ROWS]
        stream[:, HALF:K] += got[ROWS:PAIR]

    st = stream[...]
    y = bf(st * gain_ref[...])
    y_all[i] = jnp.concatenate([y[:, 0:HALF], y[:, HALF:K]], axis=0)
    ss_all[i] = jnp.broadcast_to(jnp.sum(st * st, axis=1, keepdims=True), (ROWS, LANE))
    for d in (2, 1, 3):
        dev = (g, (i + d) % N, j)
        remote(y_all.at[i], y_all.at[i], y_ss.at[d], y_rs.at[i], dev).start()
        remote(ss_all.at[i], ss_all.at[i], q_ss.at[d], q_rs.at[i], dev).start()
    for d in (1, 3, 2):
        s = (i + d) % N
        remote(meta_all.at[s], meta_all.at[s], m_ss.at[d], m_rs.at[s], sibling).wait_recv()
        remote(ss_all.at[s], ss_all.at[s], q_ss.at[d], q_rs.at[s], sibling).wait_recv()
        remote(y_all.at[s], y_all.at[s], y_ss.at[d], y_rs.at[s], sibling).wait_recv()

    ydat = [
        jnp.concatenate([y_all[k, ROWS * h : ROWS * (h + 1), :] for k in range(N)], axis=0)
        for h in range(2)
    ]
    ssd = jnp.concatenate([ss_all[k] for k in range(N)], axis=0)
    twice = bf(
        lax.broadcasted_iota(jnp.int32, (LANE, 2 * LANE), 1) // 2
        == lax.broadcasted_iota(jnp.int32, (LANE, 2 * LANE), 0)
    )
    keep = (
        lax.broadcasted_iota(jnp.int32, (2 * SLOTS, 2 * LANE), 1) % 2
        == lax.broadcasted_iota(jnp.int32, (2 * SLOTS, 2 * LANE), 0) // SLOTS
    )

    def spots(e):
        return jnp.concatenate(
            [meta_all[k, ROWS * e : ROWS * (e + 1), :] for k in range(N)], axis=0
        )

    for e in range(EXP_WIN):
        place = spots(e)
        place_t = jnp.transpose(
            jnp.concatenate([place, jnp.zeros((LANE - N * ROWS, LANE), jnp.float32)], axis=0)
        )[0 : 2 * SLOTS, 0 : N * ROWS]
        s_mine[e] = jnp.dot(
            place_t, ssd, precision=lax.Precision.HIGHEST, preferred_element_type=jnp.float32
        )
        place_b = bf(place_t)
        for h in range(2):
            rows = bf(mm(place_b, ydat[h]))
            for q in range(HALF // LANE):
                both = mm(rows[:, LANE * q : LANE * (q + 1)], twice)
                at = 2 * (HALF * h + LANE * q)
                xp[e, :, at : at + 2 * LANE] = bf(jnp.where(keep, both, 0.0))

    s_one = remote(s_mine.at[1 - c], s_recv.at[0], s_ss.at[0], s_rs.at[0], sibling)
    s_one.start()

    def product(e, h, p, width):
        t = e * TILES + h * STEP + 2 * p
        w = [gu[t + k] for k in range(width)]
        w = w[0] if width == 1 else jnp.concatenate(w, axis=1)
        return mm(xp[e], w)

    def sweep(e, h, store):
        @pl.loop(0, SIDE // 2)
        def _(p):
            at = pl.ds(pl.multiple_of(p * 2 * LANE, 2 * LANE), 2 * LANE)
            store(p, at, product(e, h, p, 2))

        store(SIDE // 2, pl.ds((SIDE - 1) * LANE, LANE), product(e, h, SIDE // 2, 1))

    def arrive(e):
        @pl.loop(0, TILES)
        def _(t):
            gu_copy(e, t).wait()

    arrive(1 - c)
    for n, h in enumerate((1 - x, x)):

        def to_sibling(p, at, r, n=n):
            l1_send[n, :, at] = bf(r)

        sweep(1 - c, h, to_sibling)
        remote(l1_send.at[n], l1_recv.at[n], l1_ss.at[n], l1_rs.at[n], sibling).start()
    arrive(c)
    s_one.wait_recv()
    s_mine[c] = s_mine[c] + s_recv[0]
    s_two = remote(s_mine.at[c], s_recv.at[1], s_ss.at[1], s_rs.at[1], across)
    s_two.start()
    first = remote(l1_send.at[0], l1_recv.at[0], l1_ss.at[0], l1_rs.at[0], sibling)
    first.wait_recv()

    def l2(p, at):
        return remote(l2_send.at[:, at], l2_recv.at[:, at], l2_ss.at[p], l2_rs.at[p], across)

    def h_acr(p, at, side):
        ref = hid.at[c, side, :, at]
        return remote(ref, ref, h_ss.at[p], h_rs.at[p], across)

    def h_fwd(p, at, e):
        ref = hid.at[e, 1 - x, :, at]
        return remote(ref, ref, f_ss.at[p], f_rs.at[p], sibling)

    def each(do):
        @pl.loop(0, SIDE // 2)
        def _(p):
            do(p, pl.ds(pl.multiple_of(p * 2 * LANE, 2 * LANE), 2 * LANE), 2 * LANE)

        do(SIDE // 2, pl.ds((SIDE - 1) * LANE, LANE), LANE)

    def to_across(p, at, r):
        l2_send[:, at] = bf(r + f32(l1_recv[0, :, at]))
        l2(p, at).start()

    sweep(c, 1 - x, to_across)
    second = remote(l1_send.at[1], l1_recv.at[1], l1_ss.at[1], l1_rs.at[1], sibling)
    second.wait_recv()

    def to_own(p, at, r):
        acc[:, at] = r + f32(l1_recv[1, :, at])

    sweep(c, x, to_own)
    s_two.wait_recv()
    scale = lax.rsqrt((s_mine[c] + s_recv[1])[0:SLOTS, 0:1] / D + 1e-05)

    def activate(p, at, width):
        l2(p, at).wait_recv()
        total = acc[:, at] + f32(l2_recv[:, at])
        gate, up = total[0:SLOTS] * scale, total[SLOTS : 2 * SLOTS] * scale
        value = gate / (1.0 + jnp.exp(-gate)) * up
        column = lax.broadcasted_iota(jnp.int32, (SLOTS, width), 1) + p * 2 * LANE
        value = jnp.where(jnp.logical_and(x == 1, column < LANE), 0.0, value)
        hid[c, x, :, at] = bf(
            jnp.concatenate([value, jnp.zeros((64 - SLOTS, width), jnp.float32)], axis=0)
        )
        h_acr(p, at, x).start()

    each(activate)
    h_sib = remote(hid.at[c, x], hid.at[c, x], hs_ss, hs_rs, sibling)
    h_sib.start()
    for e in range(EXP_WIN):
        wd_copy(e).wait()

    def down(e, h, n):
        rows = pl.ds(pl.multiple_of(h * STEP * LANE, LANE), WIDE)
        return mm(hid[e, h], wd[e, rows, 512 * n : 512 * (n + 1)])

    for n in range(3):
        outs[c, :, 512 * n : 512 * (n + 1)] = down(c, x, n)
    h_sib.wait_recv()
    for n in range(3):
        outs[1 - c, :, 512 * n : 512 * (n + 1)] = down(1 - c, x, n)

    def forward(p, at, width):
        h_acr(p, at, 1 - x).wait_recv()
        h_fwd(p, at, c).start()

    each(forward)
    for n in range(3):
        outs[c, :, 512 * n : 512 * (n + 1)] += down(c, 1 - x, n)
    each(lambda p, at, width: h_fwd(p, at, 1 - c).wait_recv())
    for n in range(3):
        outs[1 - c, :, 512 * n : 512 * (n + 1)] += down(1 - c, 1 - x, n)

    gates = jnp.concatenate([meta_all[k, 2 * ROWS : 3 * ROWS, :] for k in range(N)], axis=0)
    live = lax.broadcasted_iota(jnp.int32, (N * ROWS, 64), 1) < SLOTS
    picks = [bf(jnp.where(live, spots(e)[:, 0:64], 0.0)) for e in range(EXP_WIN)]
    for n in range(2):
        cols = slice(HALF * n, HALF * (n + 1))
        r = gates[:, 0:1] * mm(picks[0], bf(outs[0, :, cols]))
        r = r + gates[:, 1:2] * mm(picks[1], bf(outs[1, :, cols]))
        part[:, cols] = r
        for k in range(N):
            c_send[k, ROWS * n : ROWS * (n + 1), :] = bf(r[ROWS * k : ROWS * (k + 1), :])
    for d in (2, 1, 3):
        k = (i + d) % N
        remote(c_send.at[k], c_recv.at[i], c_ss.at[d], c_rs.at[i], (g, k, j)).start()
    stream[...] += part[mine, :]
    for d in (1, 3, 2):
        s = (i + d) % N
        remote(c_send.at[s], c_recv.at[s], c_ss.at[d], c_rs.at[s], sibling).wait_recv()
        got = f32(c_recv[s])
        stream[:, 0:HALF] += got[0:ROWS]
        stream[:, HALF:K] += got[ROWS:PAIR]
    out_ref[...] = bf(stream[...])

    for d in (1, 2, 3):
        remote(a_send, a_recv.at[i], a_ss.at[d], a_rs.at[i], sibling).wait_send()
        remote(meta_all.at[i], meta_all.at[i], m_ss.at[d], m_rs.at[i], sibling).wait_send()
        k = (i + d) % N
        remote(rs_send.at[k], rs_recv.at[i], rs_ss.at[d], rs_rs.at[i], sibling).wait_send()
        remote(y_all.at[i], y_all.at[i], y_ss.at[d], y_rs.at[i], sibling).wait_send()
        remote(ss_all.at[i], ss_all.at[i], q_ss.at[d], q_rs.at[i], sibling).wait_send()
        remote(c_send.at[k], c_recv.at[i], c_ss.at[d], c_rs.at[i], sibling).wait_send()

    @pl.when(i != j)
    def _():
        remote(a_send, a_recv.at[i], a_ss.at[0], a_rs.at[i], sibling).wait_send()

    for copy in (s_one, s_two, first, second, h_sib):
        copy.wait_send()

    def left(p, at, width):
        l2(p, at).wait_send()
        h_acr(p, at, x).wait_send()
        h_fwd(p, at, c).wait_send()

    each(left)


def attention(queries, cached_key_rows, cached_value_rows, lengths):
    row_count = queries.shape[0]
    head_count = queries.shape[1] // HEAD_WIDTH
    kv_count = cached_key_rows.shape[2] // HEAD_WIDTH
    query_group_width = head_count // kv_count
    cache_len = cached_key_rows.shape[1]
    per_head_queries = queries.reshape(row_count, kv_count, query_group_width, HEAD_WIDTH)
    per_head_keys = cached_key_rows.reshape(row_count, cache_len, kv_count, HEAD_WIDTH)
    per_head_values = cached_value_rows.reshape(row_count, cache_len, kv_count, HEAD_WIDTH)
    scores = jnp.einsum(
        "tkgd,tskd->tkgs", per_head_queries, per_head_keys, preferred_element_type=jnp.float32
    ) * HEAD_WIDTH ** (-0.5)
    live = jnp.arange(cache_len, dtype=jnp.int32)[None, :] < lengths[:, None]
    scores = jnp.where(live[:, None, None, :], scores, -1e30)
    row_max = jnp.max(scores, axis=-1, keepdims=True)
    expon = jnp.exp(scores - row_max)
    probs = (expon / jnp.sum(expon, axis=-1, keepdims=True)).astype(jnp.bfloat16)
    weighted = jnp.einsum(
        "tkgs,tskd->tkgd", probs, per_head_values, preferred_element_type=jnp.float32
    )
    return weighted.astype(jnp.bfloat16).reshape(row_count, head_count * HEAD_WIDTH)


def placement(routes, route_gates):
    matches = routes[:, :, None] == jnp.arange(EXP_WIN, dtype=jnp.int32)[None, None, :]
    chosen = jnp.any(matches, axis=1)
    earlier = jnp.arange(ROWS)[:, None] > jnp.arange(ROWS)[None, :]
    slot = jnp.sum(earlier[:, :, None] & chosen[None, :, :], axis=1, dtype=jnp.int32)
    position = jnp.where(chosen, lax.axis_index("ep") * CAP + slot, -1)
    lanes = jnp.arange(LANE, dtype=jnp.int32)
    lanes = jnp.where(lanes < 2 * SLOTS, lanes % SLOTS, -2)
    spots = (position.T[:, :, None] == lanes[None, None, :]).astype(jnp.float32)
    gates = jnp.sum(route_gates[:, :, None] * matches.astype(jnp.float32), axis=1)
    gates = jnp.pad(gates, ((0, 0), (0, LANE - EXP_WIN)))
    return jnp.concatenate([spots.reshape(EXP_WIN * ROWS, LANE), gates], axis=0)


def fused_local(
    queries,
    cached_key_rows,
    cached_value_rows,
    lengths,
    out_weight,
    residual,
    norm_gain,
    routes,
    route_gates,
    gate_up_weight,
    down_weight,
):
    attended = attention(queries, cached_key_rows, cached_value_rows, lengths)
    meta = placement(routes, route_gates)
    b16, f4 = jnp.bfloat16, jnp.float32
    vmem, hbm = pl.BlockSpec(memory_space=pltpu.VMEM), pl.BlockSpec(memory_space=pl.ANY)
    dma = pltpu.SemaphoreType.DMA
    scratch = [
        pltpu.VMEM((K, K), b16),
        pltpu.VMEM((EXP_WIN * TILES, 2 * K, LANE), b16),
        pltpu.VMEM((EXP_WIN, TILES * LANE, K), b16),
        pltpu.VMEM((PAIR, HALF), b16),
        pltpu.VMEM((N, PAIR, HALF), b16),
        pltpu.VMEM((N * ROWS, K), f4),
        pltpu.VMEM((N, PAIR, HALF), b16),
        pltpu.VMEM((N, PAIR, HALF), b16),
        pltpu.VMEM((N, 3 * ROWS, LANE), f4),
        pltpu.VMEM((N, PAIR, HALF), b16),
        pltpu.VMEM((N, ROWS, LANE), f4),
        pltpu.VMEM((ROWS, K), f4),
        pltpu.VMEM((EXP_WIN, 2 * SLOTS, 2 * K), b16),
        pltpu.VMEM((EXP_WIN, 2 * SLOTS, LANE), f4),
        pltpu.VMEM((2, 2 * SLOTS, LANE), f4),
        pltpu.VMEM((2, 2 * SLOTS, WIDE), b16),
        pltpu.VMEM((2, 2 * SLOTS, WIDE), b16),
        pltpu.VMEM((2 * SLOTS, WIDE), f4),
        pltpu.VMEM((2 * SLOTS, WIDE), b16),
        pltpu.VMEM((2 * SLOTS, WIDE), b16),
        pltpu.VMEM((EXP_WIN, 2, 64, WIDE), b16),
        pltpu.VMEM((EXP_WIN, 64, K), f4),
        pltpu.VMEM((N, PAIR, HALF), b16),
        pltpu.VMEM((N, PAIR, HALF), b16),
        dma,
        dma((EXP_WIN * TILES,)),
        dma((EXP_WIN,)),
    ]
    scratch += [dma((N,))] * 10 + [dma((2,))] * 4 + [dma((6,))] * 2
    scratch += [dma, dma] + [dma((6,))] * 4 + [dma((N,))] * 2
    return pl.pallas_call(
        fused,
        out_shape=jax.ShapeDtypeStruct((ROWS, K), b16),
        in_specs=[vmem] * 4 + [hbm] * 3,
        out_specs=vmem,
        scratch_shapes=scratch,
        compiler_params=pltpu.CompilerParams(
            collective_id=0, has_side_effects=True, vmem_limit_bytes=VMEM_BYTES
        ),
    )(attended, meta, residual, norm_gain[None, :], out_weight, gate_up_weight, down_weight)


VMEM_BYTES = 63 << 20


def pick(mesh):
    fits = mesh.shape["ep"] == N and mesh.shape["tp"] == N
    return fused_local if fits else local


def solution(mesh):
    in_specs = (
        P(("groups", "ep"), "tp"),
        P(("groups", "ep"), None, "tp"),
        P(("groups", "ep"), None, "tp"),
        P(("groups", "ep")),
        P("ep", "tp"),
        P(("groups", "ep"), "tp"),
        P("tp"),
        P(("groups", "ep"), None),
        P(("groups", "ep"), None),
        P(None, "tp", None, "ep"),
        P(None, "ep", "tp"),
    )
    out_specs = P(("groups", "ep"), "tp")
    return jax.shard_map(pick(mesh), mesh=mesh, in_specs=in_specs, out_specs=out_specs, check_vma=False)
```

```python
import jax
import jax.numpy as jnp
from jax import lax
from jax.experimental import pallas as pl
from jax.experimental.pallas import tpu as pltpu
from jax.sharding import PartitionSpec as P

D = 6144
HEAD_WIDTH = 128
EXP_WIN = 2
CAP = 14


def local(
    queries,
    cached_key_rows,
    cached_value_rows,
    lengths,
    out_weight,
    residual,
    norm_gain,
    routes,
    route_gates,
    gate_up_weight,
    down_weight,
):
    row_count = queries.shape[0]
    head_count = queries.shape[1] // HEAD_WIDTH
    kv_count = cached_key_rows.shape[2] // HEAD_WIDTH
    query_group_width = head_count // kv_count
    cache_len = cached_key_rows.shape[1]
    per_head_queries = queries.reshape(row_count, kv_count, query_group_width, HEAD_WIDTH)
    per_head_keys = cached_key_rows.reshape(row_count, cache_len, kv_count, HEAD_WIDTH)
    per_head_values = cached_value_rows.reshape(row_count, cache_len, kv_count, HEAD_WIDTH)
    scores = jnp.einsum(
        "tkgd,tskd->tkgs", per_head_queries, per_head_keys, preferred_element_type=jnp.float32
    ) * HEAD_WIDTH ** (-0.5)
    live = jnp.arange(cache_len, dtype=jnp.int32)[None, :] < lengths[:, None]
    scores = jnp.where(live[:, None, None, :], scores, -1e30)
    row_max = jnp.max(scores, axis=-1, keepdims=True)
    expon = jnp.exp(scores - row_max)
    probs = (expon / jnp.sum(expon, axis=-1, keepdims=True)).astype(jnp.bfloat16)
    weighted = jnp.einsum(
        "tkgs,tskd->tkgd", probs, per_head_values, preferred_element_type=jnp.float32
    )
    attended = weighted.astype(jnp.bfloat16).reshape(row_count, head_count * HEAD_WIDTH)
    full_rows = lax.all_gather(attended, "tp", axis=1, tiled=True)
    feature_slices = lax.all_to_all(full_rows, "ep", split_axis=1, concat_axis=0, tiled=True)
    projected = lax.psum_scatter(
        jnp.dot(feature_slices, out_weight, preferred_element_type=jnp.float32).astype(
            jnp.bfloat16
        ),
        "ep",
        scatter_dimension=0,
        tiled=True,
    ).astype(jnp.float32)
    stream = residual.astype(jnp.float32) + projected
    square_total = lax.psum(jnp.sum(stream * stream, axis=-1), "tp")
    normed = (stream * lax.rsqrt(square_total[:, None] / D + 1e-05) * norm_gain[None, :]).astype(
        jnp.bfloat16
    )
    expert_ids = jnp.arange(EXP_WIN, dtype=jnp.int32)
    matches = routes[:, :, None] == expert_ids[None, None, :]
    chosen = jnp.any(matches, axis=1)
    chosen_int = chosen.astype(jnp.int32)
    slot_index = jnp.cumsum(chosen_int, axis=0) - chosen_int
    slot_ids = jnp.arange(CAP, dtype=jnp.int32)[:, None, None]
    placement_map = (chosen[None, :, :] & (slot_index[None, :, :] == slot_ids)).astype(jnp.float32)
    buffers = jnp.einsum(
        "cte,td->ced",
        placement_map.astype(jnp.bfloat16),
        normed,
        preferred_element_type=jnp.float32,
    ).astype(jnp.bfloat16)
    partial_pre = jnp.einsum(
        "ced,edgf->cegf",
        lax.all_gather(buffers, "ep", axis=0, tiled=True),
        gate_up_weight,
        preferred_element_type=jnp.float32,
    )
    summed = lax.psum(partial_pre.astype(jnp.bfloat16), "tp").astype(jnp.float32)
    hidden = (jax.nn.silu(summed[:, :, 0]) * summed[:, :, 1]).astype(jnp.bfloat16)
    expert_out = lax.psum_scatter(
        jnp.einsum("cef,efd->ced", hidden, down_weight, preferred_element_type=jnp.float32).astype(
            jnp.bfloat16
        ),
        "ep",
        scatter_dimension=0,
        tiled=True,
    ).astype(jnp.float32)
    gate_weights = jnp.sum(route_gates[:, :, None] * matches.astype(jnp.float32), axis=1)
    combined = jnp.einsum(
        "cte,ced->td",
        placement_map * gate_weights[None, :, :],
        expert_out,
        precision=lax.Precision.HIGHEST,
    )
    return (stream + combined).astype(jnp.bfloat16)


MESH = pl.DeviceIdType.MESH
ROWS = 24
PAIR = 2 * ROWS
HALF = 768
N = 4
SLOTS = N * CAP
LANE = 128
TILES = 21
SIDE = 11
STEP = 10
WIDE = SIDE * LANE
K = 2 * HALF


def bf(x):
    return x.astype(jnp.bfloat16)


def f32(x):
    return x.astype(jnp.float32)


def mm(a, b):
    return jnp.dot(a, b, preferred_element_type=jnp.float32)


def fused(
    att_ref,
    meta_ref,
    res_ref,
    gain_ref,
    wo_hbm,
    gu_hbm,
    wd_hbm,
    out_ref,
    wo,
    gu,
    wd,
    a_send,
    a_recv,
    part,
    rs_send,
    rs_recv,
    meta_all,
    y_all,
    ss_all,
    stream,
    xp,
    s_mine,
    s_recv,
    l1_send,
    l1_recv,
    acc,
    l2_send,
    l2_recv,
    hid,
    outs,
    c_send,
    c_recv,
    wo_sem,
    gu_sem,
    wd_sem,
    a_ss,
    a_rs,
    m_ss,
    m_rs,
    rs_ss,
    rs_rs,
    y_ss,
    y_rs,
    q_ss,
    q_rs,
    s_ss,
    s_rs,
    l1_ss,
    l1_rs,
    l2_ss,
    l2_rs,
    hs_ss,
    hs_rs,
    h_ss,
    h_rs,
    f_ss,
    f_rs,
    c_ss,
    c_rs,
):
    g, i, j = lax.axis_index("groups"), lax.axis_index("ep"), lax.axis_index("tp")
    x, c = j // 2, j % 2
    sibling = (g, i, x * 2 + (1 - c))
    across = (g, i, (1 - x) * 2 + c)

    def remote(src, dst, ss, rs, dev):
        return pltpu.make_async_remote_copy(
            src_ref=src, dst_ref=dst, send_sem=ss, recv_sem=rs, device_id=dev, device_id_type=MESH
        )

    barrier = pltpu.get_barrier_semaphore()
    me = i * N + j
    for d in range(1, N * N):
        other = (me + d) % (N * N)
        pl.semaphore_signal(
            barrier, inc=1, device_id=(g, other // N, other % N), device_id_type=MESH
        )

    wo_copy = pltpu.make_async_copy(wo_hbm, wo, wo_sem)
    wo_copy.start()
    gu_flat = gu_hbm.reshape(EXP_WIN * 2 * K, TILES * LANE)

    def gu_copy(e, t):
        return pltpu.make_async_copy(
            gu_flat.at[
                pl.ds(pl.multiple_of(e * 2 * K, 2 * K), 2 * K),
                pl.ds(pl.multiple_of(t * LANE, LANE), LANE),
            ],
            gu.at[e * TILES + t],
            gu_sem.at[e * TILES + t],
        )

    def wd_copy(e):
        return pltpu.make_async_copy(wd_hbm.at[e], wd.at[e], wd_sem.at[e])

    for e in (1 - c, c):

        @pl.loop(0, TILES)
        def _(t, e=e):
            gu_copy(e, t).start()

    for e in range(EXP_WIN):
        wd_copy(e).start()

    a_send[0:ROWS, :] = att_ref[:, 0:HALF]
    a_send[ROWS:PAIR, :] = att_ref[:, HALF:K]
    meta_all[i] = meta_ref[...]

    pl.semaphore_wait(barrier, N * N - 1)

    for d in (1, 2, 3):
        remote(a_send, a_recv.at[i], a_ss.at[d], a_rs.at[i], (g, j, (j + d) % N)).start()

    @pl.when(i != j)
    def _():
        remote(a_send, a_recv.at[i], a_ss.at[0], a_rs.at[i], (g, j, j)).start()

    @pl.when(i == j)
    def _():
        a_recv[i] = a_send[...]

    for d in (1, 2, 3):
        remote(
            meta_all.at[i], meta_all.at[i], m_ss.at[d], m_rs.at[i], (g, (i + d) % N, j)
        ).start()

    for d in range(N):
        s = (i + d) % N

        @pl.when(jnp.logical_or(d != 0, i != j))
        def _(s=s):
            remote(a_send, a_recv.at[s], a_ss.at[0], a_rs.at[s], sibling).wait_recv()

    wo_copy.wait()
    lhs = [
        jnp.concatenate([a_recv[k, ROWS * h : ROWS * (h + 1), :] for k in range(N)], axis=0)
        for h in range(2)
    ]
    for n in range(2):
        cols = slice(HALF * n, HALF * (n + 1))
        r = mm(lhs[0], wo[0:HALF, cols]) + mm(lhs[1], wo[HALF:K, cols])
        part[:, cols] = r
        for k in range(N):
            rs_send[k, ROWS * n : ROWS * (n + 1), :] = bf(r[ROWS * k : ROWS * (k + 1), :])
    for d in (2, 1, 3):
        k = (i + d) % N
        remote(rs_send.at[k], rs_recv.at[i], rs_ss.at[d], rs_rs.at[i], (g, k, j)).start()
    mine = pl.ds(pl.multiple_of(i * ROWS, 8), ROWS)
    stream[...] = f32(res_ref[...]) + part[mine, :]
    for d in (1, 3, 2):
        s = (i + d) % N
        remote(meta_all.at[s], meta_all.at[s], m_ss.at[d], m_rs.at[s], sibling).wait_recv()
    gain = jnp.concatenate([gain_ref[q : q + 1, :] for q in range(K // LANE)], axis=1)
    twice = bf(
        lax.broadcasted_iota(jnp.int32, (LANE, 2 * LANE), 1) // 2
        == lax.broadcasted_iota(jnp.int32, (LANE, 2 * LANE), 0)
    )
    keep = (
        lax.broadcasted_iota(jnp.int32, (2 * SLOTS, 2 * LANE), 1) % 2
        == lax.broadcasted_iota(jnp.int32, (2 * SLOTS, 2 * LANE), 0) // SLOTS
    )

    def spots(e):
        return jnp.concatenate(
            [meta_all[k, ROWS * e : ROWS * (e + 1), :] for k in range(N)], axis=0
        )

    fill = jnp.zeros((LANE - N * ROWS, LANE), jnp.float32)
    places = [
        jnp.transpose(jnp.concatenate([spots(e), fill], axis=0))[0 : 2 * SLOTS, 0 : N * ROWS]
        for e in range(EXP_WIN)
    ]
    for d in (1, 3, 2):
        s = (i + d) % N
        remote(rs_send.at[s], rs_recv.at[s], rs_ss.at[d], rs_rs.at[s], sibling).wait_recv()
        got = f32(rs_recv[s])
        stream[:, 0:HALF] += got[0:ROWS]
        stream[:, HALF:K] += got[ROWS:PAIR]

    st = stream[...]
    y = bf(st * gain)
    y_all[i] = jnp.concatenate([y[:, 0:HALF], y[:, HALF:K]], axis=0)
    ss_all[i] = jnp.broadcast_to(jnp.sum(st * st, axis=1, keepdims=True), (ROWS, LANE))
    for d in (2, 1, 3):
        dev = (g, (i + d) % N, j)
        remote(y_all.at[i], y_all.at[i], y_ss.at[d], y_rs.at[i], dev).start()
        remote(ss_all.at[i], ss_all.at[i], q_ss.at[d], q_rs.at[i], dev).start()
    for d in (1, 3, 2):
        s = (i + d) % N
        remote(ss_all.at[s], ss_all.at[s], q_ss.at[d], q_rs.at[s], sibling).wait_recv()
        remote(y_all.at[s], y_all.at[s], y_ss.at[d], y_rs.at[s], sibling).wait_recv()

    ydat = [
        jnp.concatenate([y_all[k, ROWS * h : ROWS * (h + 1), :] for k in range(N)], axis=0)
        for h in range(2)
    ]
    ssd = jnp.concatenate([ss_all[k] for k in range(N)], axis=0)
    for e in range(EXP_WIN):
        place_t = places[e]
        s_mine[e] = jnp.dot(
            place_t, ssd, precision=lax.Precision.HIGHEST, preferred_element_type=jnp.float32
        )
        place_b = bf(place_t)
        for h in range(2):
            rows = bf(mm(place_b, ydat[h]))
            for q in range(HALF // LANE):
                both = mm(rows[:, LANE * q : LANE * (q + 1)], twice)
                at = 2 * (HALF * h + LANE * q)
                xp[e, :, at : at + 2 * LANE] = bf(jnp.where(keep, both, 0.0))

    s_one = remote(s_mine.at[1 - c], s_recv.at[0], s_ss.at[0], s_rs.at[0], sibling)
    s_one.start()

    def product(e, h, p, width):
        t = e * TILES + h * STEP + 2 * p
        w = [gu[t + k] for k in range(width)]
        w = w[0] if width == 1 else jnp.concatenate(w, axis=1)
        return mm(xp[e], w)

    def sweep(e, h, store):
        @pl.loop(0, SIDE // 2)
        def _(p):
            at = pl.ds(pl.multiple_of(p * 2 * LANE, 2 * LANE), 2 * LANE)
            store(p, at, product(e, h, p, 2))

        store(SIDE // 2, pl.ds((SIDE - 1) * LANE, LANE), product(e, h, SIDE // 2, 1))

    def arrive(e):
        @pl.loop(0, TILES)
        def _(t):
            gu_copy(e, t).wait()

    arrive(1 - c)
    for n, h in enumerate((1 - x, x)):

        def to_sibling(p, at, r, n=n):
            l1_send[n, :, at] = bf(r)

        sweep(1 - c, h, to_sibling)
        remote(l1_send.at[n], l1_recv.at[n], l1_ss.at[n], l1_rs.at[n], sibling).start()
    arrive(c)
    s_one.wait_recv()
    s_mine[c] = s_mine[c] + s_recv[0]
    s_two = remote(s_mine.at[c], s_recv.at[1], s_ss.at[1], s_rs.at[1], across)
    s_two.start()
    first = remote(l1_send.at[0], l1_recv.at[0], l1_ss.at[0], l1_rs.at[0], sibling)
    first.wait_recv()

    def l2(p, at):
        return remote(l2_send.at[:, at], l2_recv.at[:, at], l2_ss.at[p], l2_rs.at[p], across)

    def h_acr(p, at, side):
        ref = hid.at[c, side, :, at]
        return remote(ref, ref, h_ss.at[p], h_rs.at[p], across)

    def h_fwd(p, at, e):
        ref = hid.at[e, 1 - x, :, at]
        return remote(ref, ref, f_ss.at[p], f_rs.at[p], sibling)

    def each(do):
        @pl.loop(0, SIDE // 2)
        def _(p):
            do(p, pl.ds(pl.multiple_of(p * 2 * LANE, 2 * LANE), 2 * LANE), 2 * LANE)

        do(SIDE // 2, pl.ds((SIDE - 1) * LANE, LANE), LANE)

    def to_across(p, at, r):
        l2_send[:, at] = bf(r + f32(l1_recv[0, :, at]))
        l2(p, at).start()

    sweep(c, 1 - x, to_across)
    second = remote(l1_send.at[1], l1_recv.at[1], l1_ss.at[1], l1_rs.at[1], sibling)
    second.wait_recv()

    def to_own(p, at, r):
        acc[:, at] = r + f32(l1_recv[1, :, at])

    sweep(c, x, to_own)
    s_two.wait_recv()
    scale = lax.rsqrt((s_mine[c] + s_recv[1])[0:SLOTS, 0:1] / D + 1e-05)

    def activate(p, at, width):
        l2(p, at).wait_recv()
        total = acc[:, at] + f32(l2_recv[:, at])
        gate, up = total[0:SLOTS] * scale, total[SLOTS : 2 * SLOTS] * scale
        value = gate / (1.0 + jnp.exp(-gate)) * up
        column = lax.broadcasted_iota(jnp.int32, (SLOTS, width), 1) + p * 2 * LANE
        value = jnp.where(jnp.logical_and(x == 1, column < LANE), 0.0, value)
        hid[c, x, :, at] = bf(
            jnp.concatenate([value, jnp.zeros((64 - SLOTS, width), jnp.float32)], axis=0)
        )
        h_acr(p, at, x).start()

    each(activate)
    h_sib = remote(hid.at[c, x], hid.at[c, x], hs_ss, hs_rs, sibling)
    h_sib.start()
    for e in range(EXP_WIN):
        wd_copy(e).wait()

    def down(e, h, n):
        rows = pl.ds(pl.multiple_of(h * STEP * LANE, LANE), WIDE)
        return mm(hid[e, h], wd[e, rows, 512 * n : 512 * (n + 1)])

    for n in range(3):
        outs[c, :, 512 * n : 512 * (n + 1)] = down(c, x, n)
    h_sib.wait_recv()
    for n in range(3):
        outs[1 - c, :, 512 * n : 512 * (n + 1)] = down(1 - c, x, n)

    def forward(p, at, width):
        h_acr(p, at, 1 - x).wait_recv()
        h_fwd(p, at, c).start()

    each(forward)
    for n in range(3):
        outs[c, :, 512 * n : 512 * (n + 1)] += down(c, 1 - x, n)
    each(lambda p, at, width: h_fwd(p, at, 1 - c).wait_recv())
    for n in range(3):
        outs[1 - c, :, 512 * n : 512 * (n + 1)] += down(1 - c, 1 - x, n)

    gates = jnp.concatenate([meta_all[k, 2 * ROWS : 3 * ROWS, :] for k in range(N)], axis=0)
    live = lax.broadcasted_iota(jnp.int32, (N * ROWS, 64), 1) < SLOTS
    picks = [bf(jnp.where(live, spots(e)[:, 0:64], 0.0)) for e in range(EXP_WIN)]
    for n in range(2):
        cols = slice(HALF * n, HALF * (n + 1))
        r = gates[:, 0:1] * mm(picks[0], bf(outs[0, :, cols]))
        r = r + gates[:, 1:2] * mm(picks[1], bf(outs[1, :, cols]))
        part[:, cols] = r
        for k in range(N):
            c_send[k, ROWS * n : ROWS * (n + 1), :] = bf(r[ROWS * k : ROWS * (k + 1), :])
    for d in (2, 1, 3):
        k = (i + d) % N
        remote(c_send.at[k], c_recv.at[i], c_ss.at[d], c_rs.at[i], (g, k, j)).start()
    stream[...] += part[mine, :]
    for d in (1, 3, 2):
        s = (i + d) % N
        remote(c_send.at[s], c_recv.at[s], c_ss.at[d], c_rs.at[s], sibling).wait_recv()
        got = f32(c_recv[s])
        stream[:, 0:HALF] += got[0:ROWS]
        stream[:, HALF:K] += got[ROWS:PAIR]
    out_ref[...] = stream[...]

    for d in (1, 2, 3):
        remote(a_send, a_recv.at[i], a_ss.at[d], a_rs.at[i], sibling).wait_send()
        remote(meta_all.at[i], meta_all.at[i], m_ss.at[d], m_rs.at[i], sibling).wait_send()
        k = (i + d) % N
        remote(rs_send.at[k], rs_recv.at[i], rs_ss.at[d], rs_rs.at[i], sibling).wait_send()
        remote(y_all.at[i], y_all.at[i], y_ss.at[d], y_rs.at[i], sibling).wait_send()
        remote(ss_all.at[i], ss_all.at[i], q_ss.at[d], q_rs.at[i], sibling).wait_send()
        remote(c_send.at[k], c_recv.at[i], c_ss.at[d], c_rs.at[i], sibling).wait_send()

    @pl.when(i != j)
    def _():
        remote(a_send, a_recv.at[i], a_ss.at[0], a_rs.at[i], sibling).wait_send()

    for copy in (s_one, s_two, first, second, h_sib):
        copy.wait_send()

    def left(p, at, width):
        l2(p, at).wait_send()
        h_acr(p, at, x).wait_send()
        h_fwd(p, at, c).wait_send()

    each(left)


def attention(queries, cached_key_rows, cached_value_rows, lengths):
    row_count = queries.shape[0]
    head_count = queries.shape[1] // HEAD_WIDTH
    kv_count = cached_key_rows.shape[2] // HEAD_WIDTH
    query_group_width = head_count // kv_count
    cache_len = cached_key_rows.shape[1]
    per_head_queries = queries.reshape(row_count, kv_count, query_group_width, HEAD_WIDTH)
    per_head_keys = cached_key_rows.reshape(row_count, cache_len, kv_count, HEAD_WIDTH)
    per_head_values = cached_value_rows.reshape(row_count, cache_len, kv_count, HEAD_WIDTH)
    scores = jnp.einsum(
        "tkgd,tskd->tkgs", per_head_queries, per_head_keys, preferred_element_type=jnp.float32
    ) * HEAD_WIDTH ** (-0.5)
    live = jnp.arange(cache_len, dtype=jnp.int32)[None, :] < lengths[:, None]
    scores = jnp.where(live[:, None, None, :], scores, -1e30)
    row_max = jnp.max(scores, axis=-1, keepdims=True)
    expon = jnp.exp(scores - row_max)
    probs = (expon / jnp.sum(expon, axis=-1, keepdims=True)).astype(jnp.bfloat16)
    weighted = jnp.einsum(
        "tkgs,tskd->tkgd", probs, per_head_values, preferred_element_type=jnp.float32
    )
    return weighted.astype(jnp.bfloat16).reshape(row_count, head_count * HEAD_WIDTH)


def placement(routes, route_gates):
    matches = routes[:, :, None] == jnp.arange(EXP_WIN, dtype=jnp.int32)[None, None, :]
    chosen = jnp.any(matches, axis=1)
    earlier = jnp.arange(ROWS)[:, None] > jnp.arange(ROWS)[None, :]
    slot = jnp.sum(earlier[:, :, None] & chosen[None, :, :], axis=1, dtype=jnp.int32)
    position = jnp.where(chosen, lax.axis_index("ep") * CAP + slot, -1)
    lanes = jnp.arange(LANE, dtype=jnp.int32)
    lanes = jnp.where(lanes < 2 * SLOTS, lanes % SLOTS, -2)
    spots = (position.T[:, :, None] == lanes[None, None, :]).astype(jnp.float32)
    gates = jnp.sum(route_gates[:, :, None] * matches.astype(jnp.float32), axis=1)
    gates = jnp.pad(gates, ((0, 0), (0, LANE - EXP_WIN)))
    return jnp.concatenate([spots.reshape(EXP_WIN * ROWS, LANE), gates], axis=0)


def fused_local(
    queries,
    cached_key_rows,
    cached_value_rows,
    lengths,
    out_weight,
    residual,
    norm_gain,
    routes,
    route_gates,
    gate_up_weight,
    down_weight,
):
    attended = attention(queries, cached_key_rows, cached_value_rows, lengths)
    meta = placement(routes, route_gates)
    b16, f4 = jnp.bfloat16, jnp.float32
    vmem, hbm = pl.BlockSpec(memory_space=pltpu.VMEM), pl.BlockSpec(memory_space=pl.ANY)
    dma = pltpu.SemaphoreType.DMA
    scratch = [
        pltpu.VMEM((K, K), b16),
        pltpu.VMEM((EXP_WIN * TILES, 2 * K, LANE), b16),
        pltpu.VMEM((EXP_WIN, TILES * LANE, K), b16),
        pltpu.VMEM((PAIR, HALF), b16),
        pltpu.VMEM((N, PAIR, HALF), b16),
        pltpu.VMEM((N * ROWS, K), f4),
        pltpu.VMEM((N, PAIR, HALF), b16),
        pltpu.VMEM((N, PAIR, HALF), b16),
        pltpu.VMEM((N, 3 * ROWS, LANE), f4),
        pltpu.VMEM((N, PAIR, HALF), b16),
        pltpu.VMEM((N, ROWS, LANE), f4),
        pltpu.VMEM((ROWS, K), f4),
        pltpu.VMEM((EXP_WIN, 2 * SLOTS, 2 * K), b16),
        pltpu.VMEM((EXP_WIN, 2 * SLOTS, LANE), f4),
        pltpu.VMEM((2, 2 * SLOTS, LANE), f4),
        pltpu.VMEM((2, 2 * SLOTS, WIDE), b16),
        pltpu.VMEM((2, 2 * SLOTS, WIDE), b16),
        pltpu.VMEM((2 * SLOTS, WIDE), f4),
        pltpu.VMEM((2 * SLOTS, WIDE), b16),
        pltpu.VMEM((2 * SLOTS, WIDE), b16),
        pltpu.VMEM((EXP_WIN, 2, 64, WIDE), b16),
        pltpu.VMEM((EXP_WIN, 64, K), f4),
        pltpu.VMEM((N, PAIR, HALF), b16),
        pltpu.VMEM((N, PAIR, HALF), b16),
        dma,
        dma((EXP_WIN * TILES,)),
        dma((EXP_WIN,)),
    ]
    scratch += [dma((N,))] * 10 + [dma((2,))] * 4 + [dma((6,))] * 2
    scratch += [dma, dma] + [dma((6,))] * 4 + [dma((N,))] * 2
    return pl.pallas_call(
        fused,
        out_shape=jax.ShapeDtypeStruct((ROWS, K), f4),
        in_specs=[vmem] * 4 + [hbm] * 3,
        out_specs=vmem,
        scratch_shapes=scratch,
        compiler_params=pltpu.CompilerParams(
            collective_id=0, has_side_effects=True, vmem_limit_bytes=VMEM_BYTES
        ),
    )(attended, meta, residual, norm_gain.reshape(K // LANE, LANE), out_weight, gate_up_weight, down_weight).astype(b16)


VMEM_BYTES = 63 << 20


def pick(mesh):
    fits = mesh.shape["ep"] == N and mesh.shape["tp"] == N
    return fused_local if fits else local


def solution(mesh):
    in_specs = (
        P(("groups", "ep"), "tp"),
        P(("groups", "ep"), None, "tp"),
        P(("groups", "ep"), None, "tp"),
        P(("groups", "ep")),
        P("ep", "tp"),
        P(("groups", "ep"), "tp"),
        P("tp"),
        P(("groups", "ep"), None),
        P(("groups", "ep"), None),
        P(None, "tp", None, "ep"),
        P(None, "ep", "tp"),
    )
    out_specs = P(("groups", "ep"), "tp")
    return jax.shard_map(pick(mesh), mesh=mesh, in_specs=in_specs, out_specs=out_specs, check_vma=False)
```
